256 devices in a mesh: dp: 8 (over z), tensor: 32 (over x, y, core).
Axes of the slice: x: 4, y: 4, z: 8, core: 2. Of those that a mesh axis runs over, the one named last changes fastest.
Arguments:
- grad: bfloat16 [8, 8192, 14336], P('dp', 'tensor'), may hold values from -20 to 20
- left_basis: bfloat16 [8192, 256], P('tensor'), may hold values from -0.0625 to 0.0625
- right_basis: bfloat16 [14336, 256], P('dp'), may hold values from -0.046875 to 0.046875
- left_stat: float32 [256, 256], replicated, may hold values from -1 to 30, as said below
- right_stat: float32 [256, 256], replicated, may hold values from -1 to 30, as said below
Outputs:
- update: bfloat16 [8192, 14336], P('tensor', 'dp')
- new_left: float32 [256, 256], replicated
- new_right: float32 [256, 256], replicated
The draws below stay inside these ranges and needn't reach their ends.
Inputs may be any that keep to these rules, and one draw needn't show every extreme that they name: `left_stat`: symmetric positive definite. `right_stat`: symmetric positive definite.
All inputs are finite; a program needn't handle non-finite values.
Results may differ from the reference program's by a relative error of at most 0.0014.
Values may be sent and summed in bfloat16 or wider, within the bound.
No kernel may reach another device: no remote copies, remote signals or barrier semaphores. Data moves between devices by JAX's collectives and lax.ppermute only.
A program may use at most 128 MiB of HBM per device.

```python
import jax
import jax.numpy as jnp
from jax import lax

D = 8192
FF = 14336
K = 256
ITERS = 6
REPLICAS = 8


def stat_matrix(key, top):
    first, second = jax.random.split(key)
    diagonal = jnp.exp(jax.random.uniform(first, (K,), jnp.float32, 0.0, jnp.log(top)))
    noise = jax.random.uniform(second, (K, K), jnp.float32, -1.0, 1.0)
    sym = 0.5 * (noise + noise.T)
    bound = 0.98 * jnp.minimum(diagonal[:, None], diagonal[None, :]) / K
    eye = jnp.eye(K, dtype=jnp.float32) > 0.5
    return jnp.where(eye, diagonal[:, None] * jnp.ones((1, K), jnp.float32), sym * bound)


def rising_scales():
    row_pos = jnp.arange(D, dtype=jnp.float32) / (D - 1)
    rep_pos = jnp.arange(REPLICAS, dtype=jnp.float32) / (REPLICAS - 1)
    row_scale = jnp.exp(jnp.log(3.0) * (row_pos - 0.5))
    rep_scale = jnp.exp(jnp.log(3.0) * (rep_pos - 0.5))
    return rep_scale[:, None, None] * row_scale[None, :, None]


def draw_grad(key, part):
    key = jax.random.fold_in(key, 5)
    first = jax.random.fold_in(key, 0)
    scales = rising_scales()
    values = jax.random.truncated_normal(first, -6.0, 6.0, (REPLICAS, D, FF), jnp.float32)
    return (values * scales).astype(jnp.bfloat16)


def draw_left_stat(key, part):
    key = jax.random.fold_in(key, 11)
    return stat_matrix(key, 10.0)


def draw_right_stat(key, part):
    key = jax.random.fold_in(key, 23)
    return stat_matrix(key, 10.0)


def levels(own_key, shape, pieces, least, high):
    level = 1.0
    for dim, parts in pieces:
        draws = jax.random.uniform(jax.random.fold_in(jax.random.fold_in(own_key, 6), dim), (parts,), jnp.float32, least / len(pieces), high / len(pieces))
        level = level * jnp.repeat(jnp.exp(draws), shape[dim] // parts).reshape((-1,) + (1,) * (len(shape) - 1 - dim))
    return level


def normal_values(stream_key, shape, deviation, limit, pieces=(), kind=jnp.bfloat16):
    drawn = jax.random.normal(stream_key, shape, jnp.float32) * deviation
    if len(pieces) > 0:
        drawn = levels(stream_key, shape, pieces, -0.22, 0.18) * drawn
    return jnp.clip(drawn, min=-limit, max=limit).astype(kind)


def setup_inputs(seed: int = 0) -> dict:
    key_of = jax.random.split(jax.random.key(seed), 6)
    return {
        "grad": draw_grad(jax.random.fold_in(key_of[5], 71), 0),
        "left_basis": normal_values(key_of[1], (D, K), D ** -0.5, 0.0625, ((0, 32),)),
        "right_basis": normal_values(key_of[2], (FF, K), FF ** -0.5, 0.046875, ((0, 8),)),
        "left_stat": draw_left_stat(jax.random.fold_in(key_of[5], 71), 0),
        "right_stat": draw_right_stat(jax.random.fold_in(key_of[5], 71), 0),
    }


HIGH = lax.Precision.HIGHEST

def matmul(a, b):
    return jnp.dot(a, b, precision=HIGH, preferred_element_type=jnp.float32)

def shrink(raw, rank):
    eye = jnp.eye(rank, dtype=jnp.float32)
    return 0.9 * raw + 0.1 * jnp.trace(raw) / rank * eye

def inv_root(stat, rank):
    eye = jnp.eye(rank, dtype=jnp.float32)
    scale = jnp.sqrt(jnp.sum(stat * stat))
    current = eye * scale ** (-0.25)
    moving = stat / scale
    for step in range(ITERS):
        factor = (5.0 * eye - moving) * 0.25
        current = matmul(current, factor)
        square = matmul(factor, factor)
        moving = matmul(square, matmul(square, moving))
    return current

def reference(grad, left_basis, right_basis, left_stat, right_stat):
    replicas = grad.shape[0]
    left_f = left_basis.astype(jnp.float32)

    def one_replica(carry, gradient):
        left_gram, right_gram, cross = carry
        coef = jnp.dot(left_basis.T, gradient, preferred_element_type=jnp.float32)
        proj = jnp.dot(gradient, right_basis, preferred_element_type=jnp.float32)
        left_gram = left_gram + matmul(coef, coef.T)
        right_gram = right_gram + matmul(proj.T, proj)
        cross = cross + matmul(left_f.T, proj)
        return ((left_gram, right_gram, cross), None)
    zeros = jnp.zeros((K, K), jnp.float32)
    (left_gram, right_gram, cross), unused = lax.scan(one_replica, (zeros, zeros, zeros), grad)
    cross = cross / replicas
    raw_left = 0.5 * left_stat + 2.0 / (replicas * FF) * left_gram
    raw_right = 0.5 * right_stat + 2.0 / (replicas * D) * right_gram
    new_left = shrink(raw_left, K)
    new_right = shrink(raw_right, K)
    middle = matmul(matmul(inv_root(new_left, K), cross), inv_root(new_right, K))
    factor = (D * FF) ** 0.5 / K
    update = matmul(matmul(left_f, middle), right_basis.astype(jnp.float32).T) * factor
    return (update.astype(jnp.bfloat16), new_left, new_right)
```

```python
import functools

import jax
import jax.numpy as jnp
from jax import lax
from jax.experimental import pallas as pl
from jax.experimental.pallas import tpu as pltpu
from jax.sharding import Mesh
from jax.sharding import PartitionSpec as P

ITERS = 6
NX = 4
NY = 4
NZ = 8
ORDER = ((2, 0), (1, 1), (2, 1), (3, 0), (1, 0), (3, 1), (0, 0), (0, 1))
EARLY = 4
F32 = jnp.float32
BF16 = jnp.bfloat16
TRANS = (((0,), (0,)), ((), ()))
PLAIN = (((1,), (0,)), ((), ()))


def dot(a, b, dims=PLAIN):
    return lax.dot_general(a, b, dims, preferred_element_type=F32)


def split(a):
    high = a.astype(BF16)
    return high, (a - high.astype(F32)).astype(BF16)


def mul(a, b, dims=PLAIN):
    return dot(a[0], b[0], dims) + (dot(a[0], b[1], dims) + dot(a[1], b[0], dims))


def params(mib):
    return pltpu.CompilerParams(vmem_limit_bytes=mib * 1024 * 1024)


def shift(x, step):
    pairs = []
    for px in range(NX):
        for py in range(NY):
            pairs.append(((px * NY + py) * 2, (((px + step) % NX) * NY + py) * 2))
            pairs.append(((px * NY + py) * 2 + 1, (px * NY + (py + step) % NY) * 2 + 1))
    return lax.ppermute(x, ("x", "y", "c"), pairs)


def shift_other(x, step):
    pairs = []
    for px in range(NX):
        for py in range(NY):
            pairs.append(((px * NY + py) * 2, (px * NY + (py + step) % NY) * 2))
            pairs.append(((px * NY + py) * 2 + 1, (((px + step) % NX) * NY + py) * 2 + 1))
    return lax.ppermute(x, ("x", "y", "c"), pairs)


def ring(x, step):
    return lax.ppermute(x, "z", [(i, (i + step) % NZ) for i in range(NZ)])


def tie(*arrays):
    return lax.optimization_barrier(arrays)


def swap(x):
    return lax.ppermute(x, "c", [(0, 1), (1, 0)])


def everyone(x, axes, size):
    return lax.all_to_all(jnp.broadcast_to(x[None], (size,) + x.shape), axes, 0, 0)


def place(block, first, per):
    owner = lax.rem(block // per - first + NX, NX)
    half = lax.rem(block, per)
    spot = jnp.int32(ORDER.index((0, 0)))
    for i, (who, which) in enumerate(ORDER):
        spot = jnp.where((owner == who) & (half == which), i, spot)
    return spot


def source(i, first, per):
    who, which = ORDER[i]
    return lax.rem(first + who, NX) * per + which


def cost(flops, moved):
    return pl.CostEstimate(flops=flops, bytes_accessed=moved, transcendentals=0)


def deal_kernel(wide, plans, where, grad, *rest):
    outs, sems = rest[:-1], rest[-1]
    core = where[0]
    copies = []
    for (own, low, high), out in zip(plans, outs):
        first = where[1] if own else where[2]
        half = core if own else 1 - core
        for i in range(low, high):
            column = pl.multiple_of((2 * source(i, first, 2) + half) * wide, 128)
            item = pltpu.make_async_copy(
                grad.at[:, pl.ds(column, wide)], out.at[:, pl.ds((i - low) * wide, wide)], sems.at[len(copies)]
            )
            item.start()
            copies.append(item)
    for item in copies:
        item.wait()


def deal(where, grad, wide, plans):
    rows = grad.shape[0]
    count = sum(high - low for _, low, high in plans)
    vmem = pl.BlockSpec(memory_space=pltpu.VMEM)
    return pl.pallas_call(
        functools.partial(deal_kernel, wide, plans),
        out_shape=tuple(jax.ShapeDtypeStruct((rows, (high - low) * wide), grad.dtype) for _, low, high in plans),
        in_specs=[pl.BlockSpec(memory_space=pltpu.SMEM), pl.BlockSpec(memory_space=pl.ANY)],
        out_specs=tuple(vmem for _ in plans),
        scratch_shapes=[pltpu.SemaphoreType.DMA((count,))],
        compiler_params=params(10),
        name="deal",
    )(where, grad)


def coef_kernel(wide, offset, keep, got, left, left_got, *outs):
    at = 0
    for out in outs:
        for row in range(0, out.shape[0], wide):
            here = pl.ds((offset + at) * wide, wide)
            there = pl.ds(at * wide, wide)
            value = dot(keep[:, here], left[...], TRANS) + dot(got[:, there], left_got[...], TRANS)
            out[row : row + wide, :] = value.astype(out.dtype)
            at += 1


def coef_call(keep, got, left, left_got, wide, offset, counts):
    rank = left.shape[1]
    vmem = pl.BlockSpec(memory_space=pltpu.VMEM)
    return pl.pallas_call(
        functools.partial(coef_kernel, wide, offset),
        out_shape=tuple(jax.ShapeDtypeStruct((n * wide, rank), BF16) for n in counts),
        in_specs=[vmem] * 4,
        out_specs=tuple(vmem for _ in counts),
        compiler_params=params(12),
        name="coef",
    )(keep, got, left, left_got)


def proj_kernel(wide, steps, where, keep, got_early, got_late, *rest):
    blocks, rest = rest[: len(steps)], rest[len(steps) :]
    mine, theirs = rest[-2:]
    if len(rest) == 4:
        mine[...] = rest[0][...]
        theirs[...] = rest[1][...]
    else:
        mine[...] = jnp.zeros_like(mine)
        theirs[...] = jnp.zeros_like(theirs)
    first, replica = where[1], where[3]
    for (step, skip), block in zip(steps, blocks):
        spot = place(lax.rem(replica + step + NZ, NZ), first, 2)
        size = block.shape[0]

        def columns(at):
            return pl.ds(pl.multiple_of(at * wide + skip, 128), size)

        mine[...] += dot(keep[:, columns(spot)], block[...])

        @pl.when(spot < EARLY)
        def _():
            theirs[...] += dot(got_early[:, columns(spot)], block[...])

        @pl.when(spot >= EARLY)
        def _():
            theirs[...] += dot(got_late[:, columns(spot - EARLY)], block[...])


def proj_call(where, keep, got_early, got_late, blocks, steps, wide, sums=()):
    rows = keep.shape[0]
    rank = blocks[0].shape[1]
    shape = jax.ShapeDtypeStruct((rows, rank), F32)
    vmem = pl.BlockSpec(memory_space=pltpu.VMEM)
    return pl.pallas_call(
        functools.partial(proj_kernel, wide, steps),
        out_shape=(shape, shape),
        in_specs=[pl.BlockSpec(memory_space=pltpu.SMEM)] + [vmem] * (3 + len(blocks) + len(sums)),
        out_specs=(vmem, vmem),
        compiler_params=params(12),
        name="proj",
    )(where, keep, got_early, got_late, *blocks, *sums)


def left_gram_kernel(c0, c1, c2, c3, out):
    coef = split(
        (c0[...].astype(F32) + c1[...].astype(F32)) + (c2[...].astype(F32) + c3[...].astype(F32))
    )
    out[...] = mul(coef, coef, TRANS)


def left_gram_call(terms):
    rank = terms[0].shape[1]
    vmem = pl.BlockSpec(memory_space=pltpu.VMEM)
    return pl.pallas_call(
        left_gram_kernel,
        out_shape=jax.ShapeDtypeStruct((rank, rank), F32),
        in_specs=[vmem] * 4,
        out_specs=vmem,
        compiler_params=params(12),
        cost_estimate=cost(6 * rank**3, 16 * rank**2),
        name="left_gram",
    )(*terms)


def gram_kernel(where, mine, theirs, left, left_part, keep, send, parts):
    rank = left.shape[1]
    half = rank // 2
    proj = split(mine[...] + theirs[...])
    basis = left[...]
    parts[:, 0:rank] = left_part[...]
    parts[:, rank : 2 * rank] = mul(proj, proj, TRANS)
    parts[:, 2 * rank :] = dot(basis, proj[0], TRANS) + dot(basis, proj[1], TRANS)
    core = where[0]
    keep[...] = parts[pl.ds(pl.multiple_of(core * half, half), half), :]
    send[...] = parts[pl.ds(pl.multiple_of((1 - core) * half, half), half), :]


def gram_call(where, mine, theirs, left, left_part):
    rank = left.shape[1]
    shape = jax.ShapeDtypeStruct((rank // 2, 3 * rank), F32)
    vmem = pl.BlockSpec(memory_space=pltpu.VMEM)
    return pl.pallas_call(
        gram_kernel,
        out_shape=(shape, shape),
        in_specs=[pl.BlockSpec(memory_space=pltpu.SMEM)] + [vmem] * 4,
        out_specs=(vmem, vmem),
        scratch_shapes=[pltpu.VMEM((rank, 3 * rank), F32)],
        compiler_params=params(12),
        cost_estimate=cost(10 * rank**3, 24 * rank**2),
        name="grams",
    )(where, mine, theirs, left, left_part)


def unit(rank):
    rows = lax.broadcasted_iota(jnp.int32, (rank, rank), 0)
    cols = lax.broadcasted_iota(jnp.int32, (rank, rank), 1)
    return (rows == cols).astype(F32)


def total(a):
    return jnp.sum(jnp.sum(a, axis=1, keepdims=True), axis=0, keepdims=True)


def roots(stats, eye):
    scales = [jnp.sqrt(total(s * s)) for s in stats]
    currents = [None] * len(stats)
    movings = [s / c for s, c in zip(stats, scales)]
    for step in range(ITERS):
        factors = [(5.0 * eye - m) * 0.25 for m in movings]
        parts = [split(f) for f in factors]
        if step == 0:
            currents = [f * lax.rsqrt(jnp.sqrt(c)) for f, c in zip(factors, scales)]
        else:
            currents = [mul(f, split(x)) for x, f in zip(currents, parts)]
        if step < ITERS - 1:
            squares = [split(mul(f, f)) for f in parts]
            firsts = [split(mul(s, split(m))) for s, m in zip(squares, movings)]
            movings = [mul(s, f) for s, f in zip(squares, firsts)]
    return currents


def final_kernel(scales, where, mine, theirs, left_stat, right_stat, left, right, update, new_left, new_right, sums):
    rank = left.shape[1]
    half = rank // 2
    core = where[0]
    sums[pl.ds(pl.multiple_of(core * half, half), half), :] = mine[...]
    sums[pl.ds(pl.multiple_of((1 - core) * half, half), half), :] = theirs[...]
    eye = unit(rank)
    news = []
    for i, stat in enumerate((left_stat, right_stat)):
        raw = 0.5 * stat[...] + scales[i] * sums[:, i * rank : (i + 1) * rank]
        news.append(0.9 * raw + (0.1 / rank) * total(raw * eye) * eye)
    new_left[...] = news[0]
    new_right[...] = news[1]
    root_left, root_right = roots(news, eye)
    cross = sums[:, 2 * rank :] * scales[2]
    middle = mul(split(mul(split(root_left), split(cross))), split(root_right))
    middle = split(middle * scales[3])
    basis = left[...]
    rotated = split(dot(basis, middle[0]) + dot(basis, middle[1]))
    other = right[...]
    dims = (((1,), (1,)), ((), ()))
    update[...] = (dot(rotated[0], other, dims) + dot(rotated[1], other, dims)).astype(update.dtype)


def final_call(scales, where, mine, theirs, left_stat, right_stat, left, right):
    rank = left.shape[1]
    vmem = pl.BlockSpec(memory_space=pltpu.VMEM)
    small = jax.ShapeDtypeStruct((rank, rank), F32)
    return pl.pallas_call(
        functools.partial(final_kernel, scales),
        out_shape=(jax.ShapeDtypeStruct((left.shape[0], right.shape[0]), BF16), small, small),
        in_specs=[pl.BlockSpec(memory_space=pltpu.SMEM)] + [vmem] * 6,
        out_specs=(vmem, vmem, vmem),
        scratch_shapes=[pltpu.VMEM((rank, 3 * rank), F32)],
        compiler_params=params(12),
        name="roots_and_update",
    )(where, mine, theirs, left_stat, right_stat, left, right)


def local(grad, left_basis, right_basis, left_stat, right_stat):
    gradient = grad[0]
    rows, width = gradient.shape
    rank = left_basis.shape[1]
    replicas = lax.axis_size("z")
    groups = lax.axis_size(("x", "y", "c"))
    core = lax.axis_index("c")
    px, py = lax.axis_index("x"), lax.axis_index("y")
    first = jnp.where(core == 0, px, py)
    second = jnp.where(core == 0, py, px)
    first_other = jnp.where(core == 0, py, px)
    where = jnp.stack([core, first, first_other, lax.axis_index("z")]).astype(jnp.int32)

    wide = width // (2 * replicas)

    def proj(blocks, steps, sums=()):
        return proj_call(where, keep, got_early, got_late, blocks, steps, wide, sums)

    own = lax.dynamic_index_in_dim(right_basis.reshape(2, wide, rank), core, 0, keepdims=False)
    gradient, own = tie(gradient, own)
    up1, down1 = ring(own, 1), ring(own, -1)
    (send_early,) = deal(where, gradient, wide, ((False, 0, EARLY),))
    got_early = swap(send_early)
    left_got = swap(left_basis)
    (send_late,) = deal(where, gradient, wide, ((False, EARLY, len(ORDER)),))
    got_late = swap(send_late)
    gradient, left_got = tie(gradient, left_got)
    (keep,) = deal(where, gradient, wide, ((True, 0, len(ORDER)),))

    up, down = coef_call(keep, got_early, left_basis, left_got, wide, 0, (2, 2))
    up1, down1, up, down = tie(up1, down1, up, down)
    up, down = shift(up, 1), shift(down, -1)
    up2, down2 = ring(up1, 1), ring(down1, -1)
    got_late, up1, down1 = tie(got_late, up1, down1)
    up_rest, down_rest, held = coef_call(keep, got_late, left_basis, left_got, wide, EARLY, (1, 1, 2))
    sums = proj([own, up1, down1], ((0, 0), (-1, 0), (1, 0)))
    up2, down2, up_rest, down_rest, *sums = tie(up2, down2, up_rest, down_rest, *sums)

    up3, down3 = ring(up2, 1), ring(down2, -1)
    up, down, up2, down2 = tie(up, down, up2, down2)
    up_rest = shift(up_rest + up[:wide], 1)
    down_rest = shift(down_rest + down[:wide], -1)
    sums = proj([up2, down2], ((-2, 0), (2, 0)), sums)
    up3, down3, *sums = tie(up3, down3, *sums)

    cut = (wide // 2 + 127) // 128 * 128
    far_low, far_high = ring(up3[:cut], 1), ring(down3[cut:], -1)
    up_rest, down_rest, up3, down3 = tie(up_rest, down_rest, up3, down3)
    low = held[:wide].astype(F32) + down[wide:].astype(F32) + up_rest.astype(F32)
    high = held[wide:].astype(F32) + up[wide:].astype(F32) + down_rest.astype(F32)
    held = jnp.concatenate([low, high]).astype(BF16).reshape(NY, -1, rank)

    def owner(k):
        return lax.dynamic_index_in_dim(held, lax.rem(second + k, NY), 0, keepdims=False)

    terms = [owner(0)] + [shift_other(owner(k), k) for k in range(1, NY)]
    sums = proj([up3, down3], ((-3, 0), (3, 0)), sums)
    far_low, far_high, *sums = tie(far_low, far_high, *sums)
    *terms, far_low, far_high = tie(*terms, far_low, far_high)
    left_part = left_gram_call(terms)
    mine, theirs = proj([far_low, far_high], ((NZ // 2, 0), (NZ // 2, cut)), sums)
    stay, send = gram_call(where, mine, swap(theirs), left_basis, left_part)
    plane = NX * NY
    halves = (stay + swap(send)).reshape(plane, -1, 3 * rank)
    rows_sum = jnp.sum(lax.all_to_all(halves, ("x", "y"), 0, 0), axis=0)
    rows_sum = jnp.sum(everyone(rows_sum, "z", replicas), axis=0)
    sums = everyone(rows_sum, ("x", "y"), plane).reshape(-1, 3 * rank)
    scales = (
        2.0 / (replicas * width),
        2.0 / (replicas * rows * groups),
        1.0 / replicas,
        (rows * groups * width) ** 0.5 / rank,
    )
    return final_call(scales, where, sums, swap(sums), left_stat, right_stat, left_basis, right_basis)


def solution(mesh):
    tensor = ("x", "y", "c")
    fine = Mesh(mesh.devices.reshape(mesh.shape["dp"], NX, NY, 2), ("z",) + tensor)
    in_specs = (P("z", tensor, None), P(tensor, None), P("z", None), P(), P())
    out_specs = (P(tensor, "z"), P(), P())
    return jax.shard_map(local, mesh=fine, in_specs=in_specs, out_specs=out_specs, check_vma=False)
```

```python
import functools

import jax
import jax.numpy as jnp
from jax import lax
from jax.experimental import pallas as pl
from jax.experimental.pallas import tpu as pltpu
from jax.sharding import Mesh
from jax.sharding import PartitionSpec as P

ITERS = 6
NX = 4
NY = 4
NZ = 8
ORDER = ((2, 0), (1, 1), (2, 1), (3, 0), (1, 0), (3, 1), (0, 0), (0, 1))
EARLY = 4
F32 = jnp.float32
BF16 = jnp.bfloat16
TRANS = (((0,), (0,)), ((), ()))
PLAIN = (((1,), (0,)), ((), ()))


def dot(a, b, dims=PLAIN):
    return lax.dot_general(a, b, dims, preferred_element_type=F32)


def split(a):
    high = a.astype(BF16)
    return high, (a - high.astype(F32)).astype(BF16)


def mul(a, b, dims=PLAIN):
    return dot(a[0], b[0], dims) + (dot(a[0], b[1], dims) + dot(a[1], b[0], dims))


def params(mib):
    return pltpu.CompilerParams(vmem_limit_bytes=mib * 1024 * 1024)


def shift(x, step):
    pairs = []
    for px in range(NX):
        for py in range(NY):
            pairs.append(((px * NY + py) * 2, (((px + step) % NX) * NY + py) * 2))
            pairs.append(((px * NY + py) * 2 + 1, (px * NY + (py + step) % NY) * 2 + 1))
    return lax.ppermute(x, ("x", "y", "c"), pairs)


def shift_other(x, step):
    pairs = []
    for px in range(NX):
        for py in range(NY):
            pairs.append(((px * NY + py) * 2, (px * NY + (py + step) % NY) * 2))
            pairs.append(((px * NY + py) * 2 + 1, (((px + step) % NX) * NY + py) * 2 + 1))
    return lax.ppermute(x, ("x", "y", "c"), pairs)


def ring(x, step):
    return lax.ppermute(x, "z", [(i, (i + step) % NZ) for i in range(NZ)])


def tie(*arrays):
    return lax.optimization_barrier(arrays)


def swap(x):
    return lax.ppermute(x, "c", [(0, 1), (1, 0)])


def everyone(x, axes, size):
    return lax.all_to_all(jnp.broadcast_to(x[None], (size,) + x.shape), axes, 0, 0)


def place(block, first, per):
    owner = lax.rem(block // per - first + NX, NX)
    half = lax.rem(block, per)
    spot = jnp.int32(ORDER.index((0, 0)))
    for i, (who, which) in enumerate(ORDER):
        spot = jnp.where((owner == who) & (half == which), i, spot)
    return spot


def source(i, first, per):
    who, which = ORDER[i]
    return lax.rem(first + who, NX) * per + which


def cost(flops, moved):
    return pl.CostEstimate(flops=flops, bytes_accessed=moved, transcendentals=0)


def deal_kernel(wide, plans, where, grad, *rest):
    outs, sems = rest[:-1], rest[-1]
    core = where[0]
    copies = []
    for (own, low, high), out in zip(plans, outs):
        first = where[1] if own else where[2]
        half = core if own else 1 - core
        for i in range(low, high):
            column = pl.multiple_of((2 * source(i, first, 2) + half) * wide, 128)
            item = pltpu.make_async_copy(
                grad.at[:, pl.ds(column, wide)], out.at[:, pl.ds((i - low) * wide, wide)], sems.at[len(copies)]
            )
            item.start()
            copies.append(item)
    for item in copies:
        item.wait()


def deal(where, grad, wide, plans):
    rows = grad.shape[0]
    count = sum(high - low for _, low, high in plans)
    vmem = pl.BlockSpec(memory_space=pltpu.VMEM)
    return pl.pallas_call(
        functools.partial(deal_kernel, wide, plans),
        out_shape=tuple(jax.ShapeDtypeStruct((rows, (high - low) * wide), grad.dtype) for _, low, high in plans),
        in_specs=[pl.BlockSpec(memory_space=pltpu.SMEM), pl.BlockSpec(memory_space=pltpu.HBM)],
        out_specs=tuple(vmem for _ in plans),
        scratch_shapes=[pltpu.SemaphoreType.DMA((count,))],
        compiler_params=params(10),
        name="deal",
    )(where, grad)


def coef_kernel(wide, offset, keep, got, left, left_got, *outs):
    at = 0
    for out in outs:
        for row in range(0, out.shape[0], wide):
            here = pl.ds((offset + at) * wide, wide)
            value = dot(keep[:, here], left[...], TRANS) + dot(got[:, here], left_got[...], TRANS)
            out[row : row + wide, :] = value.astype(out.dtype)
            at += 1


def coef_call(keep, got, left, left_got, wide, offset, counts):
    rank = left.shape[1]
    vmem = pl.BlockSpec(memory_space=pltpu.VMEM)
    return pl.pallas_call(
        functools.partial(coef_kernel, wide, offset),
        out_shape=tuple(jax.ShapeDtypeStruct((n * wide, rank), BF16) for n in counts),
        in_specs=[vmem] * 4,
        out_specs=tuple(vmem for _ in counts),
        compiler_params=params(12),
        name="coef",
    )(keep, got, left, left_got)


def proj_kernel(wide, steps, where, keep, got, *rest):
    blocks, rest = rest[: len(steps)], rest[len(steps) :]
    mine, theirs = rest[-2:]
    if len(rest) == 4:
        mine[...] = rest[0][...]
        theirs[...] = rest[1][...]
    else:
        mine[...] = jnp.zeros_like(mine)
        theirs[...] = jnp.zeros_like(theirs)
    first, replica = where[1], where[3]
    for (step, skip), block in zip(steps, blocks):
        spot = place(lax.rem(replica + step + NZ, NZ), first, 2)
        size = block.shape[0]

        def columns(at):
            return pl.ds(pl.multiple_of(at * wide + skip, 128), size)

        mine[...] += dot(keep[:, columns(spot)], block[...])

        theirs[...] += dot(got[:, columns(spot)], block[...])


def proj_call(where, keep, got, blocks, steps, wide, sums=()):
    rows = keep.shape[0]
    rank = blocks[0].shape[1]
    shape = jax.ShapeDtypeStruct((rows, rank), F32)
    vmem = pl.BlockSpec(memory_space=pltpu.VMEM)
    return pl.pallas_call(
        functools.partial(proj_kernel, wide, steps),
        out_shape=(shape, shape),
        in_specs=[pl.BlockSpec(memory_space=pltpu.SMEM)] + [vmem] * (2 + len(blocks) + len(sums)),
        out_specs=(vmem, vmem),
        compiler_params=params(12),
        name="proj",
    )(where, keep, got, *blocks, *sums)


def left_gram_kernel(c0, c1, c2, c3, out):
    coef = split(
        (c0[...].astype(F32) + c1[...].astype(F32)) + (c2[...].astype(F32) + c3[...].astype(F32))
    )
    out[...] = mul(coef, coef, TRANS)


def left_gram_call(terms):
    rank = terms[0].shape[1]
    vmem = pl.BlockSpec(memory_space=pltpu.VMEM)
    return pl.pallas_call(
        left_gram_kernel,
        out_shape=jax.ShapeDtypeStruct((rank, rank), F32),
        in_specs=[vmem] * 4,
        out_specs=vmem,
        compiler_params=params(12),
        cost_estimate=cost(6 * rank**3, 16 * rank**2),
        name="left_gram",
    )(*terms)


def gram_kernel(where, mine, theirs, left, left_part, keep, send, parts):
    rank = left.shape[1]
    half = rank // 2
    proj = split(mine[...] + theirs[...])
    basis = left[...]
    parts[:, 0:rank] = left_part[...]
    parts[:, rank : 2 * rank] = mul(proj, proj, TRANS)
    parts[:, 2 * rank :] = dot(basis, proj[0], TRANS) + dot(basis, proj[1], TRANS)
    core = where[0]
    keep[...] = parts[pl.ds(pl.multiple_of(core * half, half), half), :]
    send[...] = parts[pl.ds(pl.multiple_of((1 - core) * half, half), half), :]


def gram_call(where, mine, theirs, left, left_part):
    rank = left.shape[1]
    shape = jax.ShapeDtypeStruct((rank // 2, 3 * rank), F32)
    vmem = pl.BlockSpec(memory_space=pltpu.VMEM)
    return pl.pallas_call(
        gram_kernel,
        out_shape=(shape, shape),
        in_specs=[pl.BlockSpec(memory_space=pltpu.SMEM)] + [vmem] * 4,
        out_specs=(vmem, vmem),
        scratch_shapes=[pltpu.VMEM((rank, 3 * rank), F32)],
        compiler_params=params(12),
        cost_estimate=cost(10 * rank**3, 24 * rank**2),
        name="grams",
    )(where, mine, theirs, left, left_part)


def unit(rank):
    rows = lax.broadcasted_iota(jnp.int32, (rank, rank), 0)
    cols = lax.broadcasted_iota(jnp.int32, (rank, rank), 1)
    return (rows == cols).astype(F32)


def total(a):
    return jnp.sum(jnp.sum(a, axis=1, keepdims=True), axis=0, keepdims=True)


def roots(stats, eye):
    scales = [jnp.sqrt(total(s * s)) for s in stats]
    currents = [None] * len(stats)
    movings = [s / c for s, c in zip(stats, scales)]
    for step in range(ITERS):
        factors = [(5.0 * eye - m) * 0.25 for m in movings]
        parts = [split(f) for f in factors]
        if step == 0:
            currents = [f * lax.rsqrt(jnp.sqrt(c)) for f, c in zip(factors, scales)]
        else:
            currents = [mul(f, split(x)) for x, f in zip(currents, parts)]
        if step < ITERS - 1:
            squares = [split(mul(f, f)) for f in parts]
            firsts = [split(mul(s, split(m))) for s, m in zip(squares, movings)]
            movings = [mul(s, f) for s, f in zip(squares, firsts)]
    return currents


def final_kernel(scales, where, mine, theirs, left_stat, right_stat, left, right, update, new_left, new_right, sums):
    rank = left.shape[1]
    half = rank // 2
    core = where[0]
    sums[pl.ds(pl.multiple_of(core * half, half), half), :] = mine[...]
    sums[pl.ds(pl.multiple_of((1 - core) * half, half), half), :] = theirs[...]
    eye = unit(rank)
    news = []
    for i, stat in enumerate((left_stat, right_stat)):
        raw = 0.5 * stat[...] + scales[i] * sums[:, i * rank : (i + 1) * rank]
        news.append(0.9 * raw + (0.1 / rank) * total(raw * eye) * eye)
    new_left[...] = news[0]
    new_right[...] = news[1]
    root_left, root_right = roots(news, eye)
    cross = sums[:, 2 * rank :] * scales[2]
    middle = mul(split(mul(split(root_left), split(cross))), split(root_right))
    middle = split(middle * scales[3])
    basis = left[...]
    rotated = split(dot(basis, middle[0]) + dot(basis, middle[1]))
    other = right[...]
    dims = (((1,), (1,)), ((), ()))
    update[...] = (dot(rotated[0], other, dims) + dot(rotated[1], other, dims)).astype(update.dtype)


def final_call(scales, where, mine, theirs, left_stat, right_stat, left, right):
    rank = left.shape[1]
    vmem = pl.BlockSpec(memory_space=pltpu.VMEM)
    small = jax.ShapeDtypeStruct((rank, rank), F32)
    return pl.pallas_call(
        functools.partial(final_kernel, scales),
        out_shape=(jax.ShapeDtypeStruct((left.shape[0], right.shape[0]), BF16), small, small),
        in_specs=[pl.BlockSpec(memory_space=pltpu.SMEM)] + [vmem] * 6,
        out_specs=(vmem, vmem, vmem),
        scratch_shapes=[pltpu.VMEM((rank, 3 * rank), F32)],
        compiler_params=params(12),
        name="roots_and_update",
    )(where, mine, theirs, left_stat, right_stat, left, right)


def local(grad, left_basis, right_basis, left_stat, right_stat):
    gradient = grad[0]
    rows, width = gradient.shape
    rank = left_basis.shape[1]
    replicas = lax.axis_size("z")
    groups = lax.axis_size(("x", "y", "c"))
    core = lax.axis_index("c")
    px, py = lax.axis_index("x"), lax.axis_index("y")
    first = jnp.where(core == 0, px, py)
    second = jnp.where(core == 0, py, px)
    first_other = jnp.where(core == 0, py, px)
    where = jnp.stack([core, first, first_other, lax.axis_index("z")]).astype(jnp.int32)

    wide = width // (2 * replicas)

    def proj(blocks, steps, sums=()):
        return proj_call(where, keep, got, blocks, steps, wide, sums)

    own = lax.dynamic_index_in_dim(right_basis.reshape(2, wide, rank), core, 0, keepdims=False)
    gradient, own = tie(gradient, own)
    up1, down1 = ring(own, 1), ring(own, -1)
    (send,) = deal(where, gradient, wide, ((False, 0, len(ORDER)),))
    got = swap(send)
    left_got = swap(left_basis)
    gradient, left_got = tie(gradient, left_got)
    (keep,) = deal(where, gradient, wide, ((True, 0, len(ORDER)),))

    up, down = coef_call(keep, got, left_basis, left_got, wide, 0, (2, 2))
    up1, down1, up, down = tie(up1, down1, up, down)
    up, down = shift(up, 1), shift(down, -1)
    up2, down2 = ring(up1, 1), ring(down1, -1)
    got, up1, down1 = tie(got, up1, down1)
    up_rest, down_rest, held = coef_call(keep, got, left_basis, left_got, wide, EARLY, (1, 1, 2))
    sums = proj([own, up1, down1], ((0, 0), (-1, 0), (1, 0)))
    up2, down2, up_rest, down_rest, *sums = tie(up2, down2, up_rest, down_rest, *sums)

    up3, down3 = ring(up2, 1), ring(down2, -1)
    up, down, up2, down2 = tie(up, down, up2, down2)
    up_rest = shift(up_rest + up[:wide], 1)
    down_rest = shift(down_rest + down[:wide], -1)
    sums = proj([up2, down2], ((-2, 0), (2, 0)), sums)
    up3, down3, *sums = tie(up3, down3, *sums)

    cut = (wide // 2 + 127) // 128 * 128
    far_low, far_high = ring(up3[:cut], 1), ring(down3[cut:], -1)
    up_rest, down_rest, up3, down3 = tie(up_rest, down_rest, up3, down3)
    low = held[:wide].astype(F32) + down[wide:].astype(F32) + up_rest.astype(F32)
    high = held[wide:].astype(F32) + up[wide:].astype(F32) + down_rest.astype(F32)
    held = jnp.concatenate([low, high]).astype(BF16).reshape(NY, -1, rank)

    def owner(k):
        return lax.dynamic_index_in_dim(held, lax.rem(second + k, NY), 0, keepdims=False)

    terms = [owner(0)] + [shift_other(owner(k), k) for k in range(1, NY)]
    sums = proj([up3, down3], ((-3, 0), (3, 0)), sums)
    far_low, far_high, *sums = tie(far_low, far_high, *sums)
    *terms, far_low, far_high = tie(*terms, far_low, far_high)
    left_part = left_gram_call(terms)
    mine, theirs = proj([far_low, far_high], ((NZ // 2, 0), (NZ // 2, cut)), sums)
    stay, send = gram_call(where, mine, swap(theirs), left_basis, left_part)
    plane = NX * NY
    halves = (stay + swap(send)).reshape(plane, -1, 3 * rank)
    rows_sum = jnp.sum(lax.all_to_all(halves, ("x", "y"), 0, 0), axis=0)
    rows_sum = jnp.sum(everyone(rows_sum, "z", replicas), axis=0)
    sums = everyone(rows_sum, ("x", "y"), plane).reshape(-1, 3 * rank)
    scales = (
        2.0 / (replicas * width),
        2.0 / (replicas * rows * groups),
        1.0 / replicas,
        (rows * groups * width) ** 0.5 / rank,
    )
    return final_call(scales, where, sums, swap(sums), left_stat, right_stat, left_basis, right_basis)


def solution(mesh):
    tensor = ("x", "y", "c")
    fine = Mesh(mesh.devices.reshape(mesh.shape["dp"], NX, NY, 2), ("z",) + tensor)
    in_specs = (P("z", tensor, None), P(tensor, None), P("z", None), P(), P())
    out_specs = (P(tensor, "z"), P(), P())
    return jax.shard_map(local, mesh=fine, in_specs=in_specs, out_specs=out_specs, check_vma=False)
```

```python
import functools

import jax
import jax.numpy as jnp
from jax import lax
from jax.experimental import pallas as pl
from jax.experimental.pallas import tpu as pltpu
from jax.sharding import Mesh
from jax.sharding import PartitionSpec as P

ITERS = 6
NX = 4
NY = 4
NZ = 8
ORDER = ((2, 0), (1, 1), (2, 1), (3, 0), (1, 0), (3, 1), (0, 0), (0, 1))
EARLY = 4
F32 = jnp.float32
BF16 = jnp.bfloat16
TRANS = (((0,), (0,)), ((), ()))
PLAIN = (((1,), (0,)), ((), ()))


def dot(a, b, dims=PLAIN):
    return lax.dot_general(a, b, dims, preferred_element_type=F32)


def split(a):
    high = a.astype(BF16)
    return high, (a - high.astype(F32)).astype(BF16)


def mul(a, b, dims=PLAIN):
    return dot(a[0], b[0], dims) + (dot(a[0], b[1], dims) + dot(a[1], b[0], dims))


def params(mib):
    return pltpu.CompilerParams(vmem_limit_bytes=mib * 1024 * 1024)


def shift(x, step):
    pairs = []
    for px in range(NX):
        for py in range(NY):
            pairs.append(((px * NY + py) * 2, (((px + step) % NX) * NY + py) * 2))
            pairs.append(((px * NY + py) * 2 + 1, (px * NY + (py + step) % NY) * 2 + 1))
    return lax.ppermute(x, ("x", "y", "c"), pairs)


def shift_other(x, step):
    pairs = []
    for px in range(NX):
        for py in range(NY):
            pairs.append(((px * NY + py) * 2, (px * NY + (py + step) % NY) * 2))
            pairs.append(((px * NY + py) * 2 + 1, (((px + step) % NX) * NY + py) * 2 + 1))
    return lax.ppermute(x, ("x", "y", "c"), pairs)


def ring(x, step):
    return lax.ppermute(x, "z", [(i, (i + step) % NZ) for i in range(NZ)])


def tie(*arrays):
    return lax.optimization_barrier(arrays)


def swap(x):
    return lax.ppermute(x, "c", [(0, 1), (1, 0)])


def everyone(x, axes, size):
    return lax.all_to_all(jnp.broadcast_to(x[None], (size,) + x.shape), axes, 0, 0)


def place(block, first, per):
    owner = lax.rem(block // per - first + NX, NX)
    half = lax.rem(block, per)
    spot = jnp.int32(ORDER.index((0, 0)))
    for i, (who, which) in enumerate(ORDER):
        spot = jnp.where((owner == who) & (half == which), i, spot)
    return spot


def source(i, first, per):
    who, which = ORDER[i]
    return lax.rem(first + who, NX) * per + which


def cost(flops, moved):
    return pl.CostEstimate(flops=flops, bytes_accessed=moved, transcendentals=0)


def deal_kernel(wide, plans, where, grad, *rest):
    outs, sems = rest[:-1], rest[-1]
    core = where[0]
    copies = []
    for (own, low, high), out in zip(plans, outs):
        first = where[1] if own else where[2]
        half = core if own else 1 - core
        for i in range(low, high):
            column = pl.multiple_of((2 * source(i, first, 2) + half) * wide, 128)
            item = pltpu.make_async_copy(
                grad.at[:, pl.ds(column, wide)], out.at[:, pl.ds((i - low) * wide, wide)], sems.at[len(copies)]
            )
            item.start()
            copies.append(item)
    for item in copies:
        item.wait()


def deal(where, grad, wide, plans, grant):
    rows = grad.shape[0]
    count = sum(high - low for _, low, high in plans)
    vmem = pl.BlockSpec(memory_space=pltpu.VMEM)
    return pl.pallas_call(
        functools.partial(deal_kernel, wide, plans),
        out_shape=tuple(jax.ShapeDtypeStruct((rows, (high - low) * wide), grad.dtype) for _, low, high in plans),
        in_specs=[pl.BlockSpec(memory_space=pltpu.SMEM), pl.BlockSpec(memory_space=pltpu.HBM)],
        out_specs=tuple(vmem for _ in plans),
        scratch_shapes=[pltpu.SemaphoreType.DMA((count,))],
        compiler_params=params(grant),
        name="deal",
    )(where, grad)


def coef_kernel(wide, offset, keep, got, left, left_got, *outs):
    at = 0
    for out in outs:
        for row in range(0, out.shape[0], wide):
            here = pl.ds((offset + at) * wide, wide)
            value = dot(keep[:, here], left[...], TRANS) + dot(got[:, here], left_got[...], TRANS)
            out[row : row + wide, :] = value.astype(out.dtype)
            at += 1


def coef_call(keep, got, left, left_got, wide, offset, counts):
    rank = left.shape[1]
    vmem = pl.BlockSpec(memory_space=pltpu.VMEM)
    return pl.pallas_call(
        functools.partial(coef_kernel, wide, offset),
        out_shape=tuple(jax.ShapeDtypeStruct((n * wide, rank), BF16) for n in counts),
        in_specs=[vmem] * 4,
        out_specs=tuple(vmem for _ in counts),
        compiler_params=params(12),
        name="coef",
    )(keep, got, left, left_got)


def proj_kernel(wide, steps, where, keep, got, *rest):
    blocks, rest = rest[: len(steps)], rest[len(steps) :]
    mine, theirs = rest[-2:]
    if len(rest) == 4:
        mine[...] = rest[0][...]
        theirs[...] = rest[1][...]
    else:
        mine[...] = jnp.zeros_like(mine)
        theirs[...] = jnp.zeros_like(theirs)
    first, replica = where[1], where[3]
    for (step, skip), block in zip(steps, blocks):
        spot = place(lax.rem(replica + step + NZ, NZ), first, 2)
        size = block.shape[0]

        def columns(at):
            return pl.ds(pl.multiple_of(at * wide + skip, 128), size)

        mine[...] += dot(keep[:, columns(spot)], block[...])

        theirs[...] += dot(got[:, columns(spot)], block[...])


def proj_call(where, keep, got, blocks, steps, wide, sums=()):
    rows = keep.shape[0]
    rank = blocks[0].shape[1]
    shape = jax.ShapeDtypeStruct((rows, rank), F32)
    vmem = pl.BlockSpec(memory_space=pltpu.VMEM)
    return pl.pallas_call(
        functools.partial(proj_kernel, wide, steps),
        out_shape=(shape, shape),
        in_specs=[pl.BlockSpec(memory_space=pltpu.SMEM)] + [vmem] * (2 + len(blocks) + len(sums)),
        out_specs=(vmem, vmem),
        compiler_params=params(12),
        name="proj",
    )(where, keep, got, *blocks, *sums)


def left_gram_kernel(c0, c1, c2, c3, out):
    coef = split(
        (c0[...].astype(F32) + c1[...].astype(F32)) + (c2[...].astype(F32) + c3[...].astype(F32))
    )
    out[...] = mul(coef, coef, TRANS)


def left_gram_call(terms):
    rank = terms[0].shape[1]
    vmem = pl.BlockSpec(memory_space=pltpu.VMEM)
    return pl.pallas_call(
        left_gram_kernel,
        out_shape=jax.ShapeDtypeStruct((rank, rank), F32),
        in_specs=[vmem] * 4,
        out_specs=vmem,
        compiler_params=params(12),
        cost_estimate=cost(6 * rank**3, 16 * rank**2),
        name="left_gram",
    )(*terms)


def gram_kernel(where, mine, theirs, left, left_part, keep, send, parts):
    rank = left.shape[1]
    half = rank // 2
    proj = split(mine[...] + theirs[...])
    basis = left[...]
    parts[:, 0:rank] = left_part[...]
    parts[:, rank : 2 * rank] = mul(proj, proj, TRANS)
    parts[:, 2 * rank :] = dot(basis, proj[0], TRANS) + dot(basis, proj[1], TRANS)
    core = where[0]
    keep[...] = parts[pl.ds(pl.multiple_of(core * half, half), half), :]
    send[...] = parts[pl.ds(pl.multiple_of((1 - core) * half, half), half), :]


def gram_call(where, mine, theirs, left, left_part):
    rank = left.shape[1]
    shape = jax.ShapeDtypeStruct((rank // 2, 3 * rank), F32)
    vmem = pl.BlockSpec(memory_space=pltpu.VMEM)
    return pl.pallas_call(
        gram_kernel,
        out_shape=(shape, shape),
        in_specs=[pl.BlockSpec(memory_space=pltpu.SMEM)] + [vmem] * 4,
        out_specs=(vmem, vmem),
        scratch_shapes=[pltpu.VMEM((rank, 3 * rank), F32)],
        compiler_params=params(12),
        cost_estimate=cost(10 * rank**3, 24 * rank**2),
        name="grams",
    )(where, mine, theirs, left, left_part)


def unit(rank):
    rows = lax.broadcasted_iota(jnp.int32, (rank, rank), 0)
    cols = lax.broadcasted_iota(jnp.int32, (rank, rank), 1)
    return (rows == cols).astype(F32)


def total(a):
    return jnp.sum(jnp.sum(a, axis=1, keepdims=True), axis=0, keepdims=True)


def roots(stats, eye):
    scales = [jnp.sqrt(total(s * s)) for s in stats]
    currents = [None] * len(stats)
    movings = [s / c for s, c in zip(stats, scales)]
    for step in range(ITERS):
        factors = [(5.0 * eye - m) * 0.25 for m in movings]
        parts = [split(f) for f in factors]
        if step == 0:
            currents = [f * lax.rsqrt(jnp.sqrt(c)) for f, c in zip(factors, scales)]
        else:
            currents = [mul(f, split(x)) for x, f in zip(currents, parts)]
        if step < ITERS - 1:
            squares = [split(mul(f, f)) for f in parts]
            firsts = [split(mul(s, split(m))) for s, m in zip(squares, movings)]
            movings = [mul(s, f) for s, f in zip(squares, firsts)]
    return currents


def final_kernel(scales, where, mine, theirs, left_stat, right_stat, left, right, update, new_left, new_right, sums):
    rank = left.shape[1]
    half = rank // 2
    core = where[0]
    sums[pl.ds(pl.multiple_of(core * half, half), half), :] = mine[...]
    sums[pl.ds(pl.multiple_of((1 - core) * half, half), half), :] = theirs[...]
    eye = unit(rank)
    news = []
    for i, stat in enumerate((left_stat, right_stat)):
        raw = 0.5 * stat[...] + scales[i] * sums[:, i * rank : (i + 1) * rank]
        news.append(0.9 * raw + (0.1 / rank) * total(raw * eye) * eye)
    new_left[...] = news[0]
    new_right[...] = news[1]
    root_left, root_right = roots(news, eye)
    cross = sums[:, 2 * rank :] * scales[2]
    middle = mul(split(mul(split(root_left), split(cross))), split(root_right))
    middle = split(middle * scales[3])
    basis = left[...]
    rotated = split(dot(basis, middle[0]) + dot(basis, middle[1]))
    other = right[...]
    dims = (((1,), (1,)), ((), ()))
    update[...] = (dot(rotated[0], other, dims) + dot(rotated[1], other, dims)).astype(update.dtype)


def final_call(scales, where, mine, theirs, left_stat, right_stat, left, right):
    rank = left.shape[1]
    vmem = pl.BlockSpec(memory_space=pltpu.VMEM)
    small = jax.ShapeDtypeStruct((rank, rank), F32)
    return pl.pallas_call(
        functools.partial(final_kernel, scales),
        out_shape=(jax.ShapeDtypeStruct((left.shape[0], right.shape[0]), BF16), small, small),
        in_specs=[pl.BlockSpec(memory_space=pltpu.SMEM)] + [vmem] * 6,
        out_specs=(vmem, vmem, vmem),
        scratch_shapes=[pltpu.VMEM((rank, 3 * rank), F32)],
        compiler_params=params(12),
        name="roots_and_update",
    )(where, mine, theirs, left_stat, right_stat, left, right)


def local(grad, left_basis, right_basis, left_stat, right_stat):
    gradient = grad[0]
    rows, width = gradient.shape
    rank = left_basis.shape[1]
    replicas = lax.axis_size("z")
    groups = lax.axis_size(("x", "y", "c"))
    core = lax.axis_index("c")
    px, py = lax.axis_index("x"), lax.axis_index("y")
    first = jnp.where(core == 0, px, py)
    second = jnp.where(core == 0, py, px)
    first_other = jnp.where(core == 0, py, px)
    where = jnp.stack([core, first, first_other, lax.axis_index("z")]).astype(jnp.int32)

    wide = width // (2 * replicas)

    def proj(blocks, steps, sums=()):
        return proj_call(where, keep, got, blocks, steps, wide, sums)

    own = lax.dynamic_index_in_dim(right_basis.reshape(2, wide, rank), core, 0, keepdims=False)
    gradient, own = tie(gradient, own)
    up1, down1 = ring(own, 1), ring(own, -1)
    (send,) = deal(where, gradient, wide, ((False, 0, len(ORDER)),), 52)
    got = swap(send)
    left_got = swap(left_basis)
    gradient, left_got = tie(gradient, left_got)
    (keep,) = deal(where, gradient, wide, ((True, 0, len(ORDER)),), 10)

    up, down = coef_call(keep, got, left_basis, left_got, wide, 0, (2, 2))
    up1, down1, up, down = tie(up1, down1, up, down)
    up, down = shift(up, 1), shift(down, -1)
    up2, down2 = ring(up1, 1), ring(down1, -1)
    got, up1, down1 = tie(got, up1, down1)
    up_rest, down_rest, held = coef_call(keep, got, left_basis, left_got, wide, EARLY, (1, 1, 2))
    sums = proj([own, up1, down1], ((0, 0), (-1, 0), (1, 0)))
    up2, down2, up_rest, down_rest, *sums = tie(up2, down2, up_rest, down_rest, *sums)

    up3, down3 = ring(up2, 1), ring(down2, -1)
    up, down, up2, down2 = tie(up, down, up2, down2)
    up_rest = shift(up_rest + up[:wide], 1)
    down_rest = shift(down_rest + down[:wide], -1)
    sums = proj([up2, down2], ((-2, 0), (2, 0)), sums)
    up3, down3, *sums = tie(up3, down3, *sums)

    cut = (wide // 2 + 127) // 128 * 128
    far_low, far_high = ring(up3[:cut], 1), ring(down3[cut:], -1)
    up_rest, down_rest, up3, down3 = tie(up_rest, down_rest, up3, down3)
    low = held[:wide].astype(F32) + down[wide:].astype(F32) + up_rest.astype(F32)
    high = held[wide:].astype(F32) + up[wide:].astype(F32) + down_rest.astype(F32)
    held = jnp.concatenate([low, high]).astype(BF16).reshape(NY, -1, rank)

    def owner(k):
        return lax.dynamic_index_in_dim(held, lax.rem(second + k, NY), 0, keepdims=False)

    terms = [owner(0)] + [shift_other(owner(k), k) for k in range(1, NY)]
    sums = proj([up3, down3], ((-3, 0), (3, 0)), sums)
    far_low, far_high, *sums = tie(far_low, far_high, *sums)
    *terms, far_low, far_high = tie(*terms, far_low, far_high)
    left_part = left_gram_call(terms)
    mine, theirs = proj([far_low, far_high], ((NZ // 2, 0), (NZ // 2, cut)), sums)
    stay, send = gram_call(where, mine, swap(theirs), left_basis, left_part)
    plane = NX * NY
    halves = (stay + swap(send)).reshape(plane, -1, 3 * rank)
    rows_sum = jnp.sum(lax.all_to_all(halves, ("x", "y"), 0, 0), axis=0)
    rows_sum = jnp.sum(everyone(rows_sum, "z", replicas), axis=0)
    sums = everyone(rows_sum, ("x", "y"), plane).reshape(-1, 3 * rank)
    scales = (
        2.0 / (replicas * width),
        2.0 / (replicas * rows * groups),
        1.0 / replicas,
        (rows * groups * width) ** 0.5 / rank,
    )
    return final_call(scales, where, sums, swap(sums), left_stat, right_stat, left_basis, right_basis)


def solution(mesh):
    tensor = ("x", "y", "c")
    fine = Mesh(mesh.devices.reshape(mesh.shape["dp"], NX, NY, 2), ("z",) + tensor)
    in_specs = (P("z", tensor, None), P(tensor, None), P("z", None), P(), P())
    out_specs = (P(tensor, "z"), P(), P())
    return jax.shard_map(local, mesh=fine, in_specs=in_specs, out_specs=out_specs, check_vma=False)
```
